32 devices in a mesh: cont: 4 (over z), line: 2 (over y), scen: 4 (over x, core).
Axes of the slice: x: 2, y: 2, z: 4, core: 2. Of those that a mesh axis runs over, the one named last changes fastest.
Arguments:
- lodf: bfloat16 [256, 4096], P('line', 'cont'), may hold values from -1 to 1
- flow: float32 [256, 256], P('line', 'scen'), may hold values from -6 to 6
- out_flow: float32 [256, 4096], P('scen', 'cont'), may hold values from -6 to 6
- limits: float32 [256], P('line'), may hold values from 0.5 to 2
- ptdf_mon: bfloat16 [256, 2048], P('line'), may hold values from -6 to 6
- ptdf_out: bfloat16 [4096, 2048], P('cont'), may hold values from -6 to 6
- viol_cont: int32 [16384], P(('cont', 'line', 'scen')), may hold values from 0 to 1023
- viol_line: int32 [16384], P(('cont', 'line', 'scen')), may hold values from 0 to 127
- viol_scen: int32 [16384], P(('cont', 'line', 'scen')), may hold values from 0 to 63
- rows_used: int32 [32], P(('cont', 'line', 'scen')), may hold values from 64 to 512, as said below
Outputs:
- worst: float32 [256, 256], P('line', 'scen')
- schur: float32 [2048, 2048], P(('line', 'scen'))
The draws below stay inside these ranges and needn't reach their ends.
Inputs may be any that keep to these rules, and one draw needn't show every extreme that they name: `rows_used`: each device uses a leading run of its 512 slots; the counts are skewed, and some device is full.
All inputs are finite; a program needn't handle non-finite values.
Results may differ from the reference program's by a relative error of at most 0.00096.
Values may be sent and summed in bfloat16 or wider, within the bound.
A program may use at most 128 MiB of HBM per device.

```python
import math
import jax
import jax.numpy as jnp
from jax import lax

K = 4096
S = 256
G = 2048
LINE_DEV = 128
ROWS_DEV = 512
L = 256
CONT_DEV = 1024
SCEN_DEV = 64
ROWS = 16384
N_LINE = 2
N_SCEN = 4
DEVICES = 32


def draw_rows_used(key, part):
    key_base = jax.random.fold_in(key, 11)
    key_full = jax.random.fold_in(key, 12)
    key_pick = jax.random.fold_in(key, 13)
    key_other = jax.random.fold_in(key, 14)
    base = jax.random.randint(key_base, (DEVICES,), ROWS_DEV // 8, ROWS_DEV // 2 + 1)
    full = jax.random.randint(key_full, (DEVICES,), 0, 8) == 0
    values = jnp.where(full, ROWS_DEV, base)
    first = jax.random.randint(key_pick, (), 0, DEVICES)
    second = (first + 1 + jax.random.randint(key_other, (), 0, DEVICES - 1)) % DEVICES
    values = values.at[first].set(ROWS_DEV)
    values = values.at[second].set(ROWS_DEV // 8)
    return values.astype(jnp.int32)


def place_ends(result, own_key, smallest, high):
    index_at = [jax.random.randint(jax.random.fold_in(own_key, axis), (), 0, length) for axis, length in enumerate(result.shape)]
    longest = result.shape.index(max(result.shape))
    beside = index_at[:longest] + [(index_at[longest] + 1) % result.shape[longest]] + index_at[longest + 1:]
    return result.at[tuple(index_at)].set(smallest).at[tuple(beside)].set(high)


def spiked(entries, key, source, target, shards_of, factor):
    def block_of(position):
        return (jnp.arange(entries.shape[position]) // (entries.shape[position] // shards_of)).reshape((-1,) + (1,) * (entries.ndim - 1 - position))

    first = jax.random.permutation(key, shards_of)[block_of(target)]
    other_side = (block_of(target) + shards_of // 2) % shards_of
    return jnp.where((block_of(source) == first) | (block_of(source) == other_side), factor * entries, entries)


def block_levels(key, extent, pieces, least, largest):
    level, own = 1.0, jax.random.fold_in(key, 6)
    for position, blocks in pieces:
        heights = jnp.exp(jax.random.uniform(jax.random.fold_in(own, position), (blocks,), jnp.float32, least / len(pieces), largest / len(pieces)))
        level = level * jnp.repeat(heights, extent[position] // blocks).reshape([-1 if axis == position else 1 for axis in range(len(extent))])
    return level


def bell_draw(own_key, dims, deviation, most, pieces=(), kind=jnp.bfloat16):
    loudness = block_levels(own_key, dims, pieces, -0.22, 0.18) if pieces else 1.0
    drawn = jax.random.normal(own_key, dims, jnp.float32) * deviation * loudness
    return jnp.minimum(jnp.maximum(drawn, -most), most).astype(kind)


def gaussian_with(rng, shape, spread, reach, split, heavy, kind=jnp.bfloat16):
    entries = spread * jax.random.normal(rng, shape, jnp.float32)
    if split:
        entries = entries * block_levels(rng, shape, split, -0.22, 0.18)
    return jnp.clip(spiked(entries, jax.random.fold_in(rng, 3), *heavy), -reach, reach).astype(kind)


def setup_inputs(seed: int = 0) -> dict:
    splits = jax.random.split(jax.random.key(seed), 11)
    lodf = jnp.clip(jax.random.uniform(splits[0], (L, K), jnp.float32, -1.0, 1.0) * block_levels(splits[0], (L, K), ((0, 2), (1, 4)), -0.4, 0.0), -1.0, 1.0).astype(jnp.bfloat16)
    flow = bell_draw(splits[1], (L, S), 1.0, 6.0, ((0, 2), (1, 4)), jnp.float32)
    out_flow = bell_draw(splits[2], (S, K), 1.0, 6.0, ((0, 4), (1, 4)), jnp.float32)
    limits = jnp.clip(jnp.exp(math.log(2.0) - 1.3862944 * jax.random.uniform(splits[3], (L,), jnp.float32) ** block_levels(splits[3], (L,), ((0, 2),), -0.2, 0.2)), 0.5, 2.0)
    ptdf_mon = gaussian_with(splits[4], (L, G), 1.0, 6.0, ((0, 2),), (0, 1, 2, 2.0))
    ptdf_out = gaussian_with(splits[5], (K, G), 1.0, 6.0, ((0, 4),), (0, 1, 4, 2.0))
    viol_cont = place_ends(jax.random.randint(splits[6], (ROWS,), 0, CONT_DEV), jax.random.fold_in(splits[6], 1), 0, CONT_DEV - 1).astype(jnp.int32)
    viol_line = place_ends(jax.random.randint(splits[7], (ROWS,), 0, LINE_DEV), jax.random.fold_in(splits[7], 1), 0, LINE_DEV - 1).astype(jnp.int32)
    viol_scen = place_ends(jax.random.randint(splits[8], (ROWS,), 0, SCEN_DEV), jax.random.fold_in(splits[8], 1), 0, SCEN_DEV - 1).astype(jnp.int32)
    rows_used = draw_rows_used(jax.random.fold_in(splits[10], 71), 0)
    return {"lodf": lodf, "flow": flow, "out_flow": out_flow, "limits": limits, "ptdf_mon": ptdf_mon, "ptdf_out": ptdf_out, "viol_cont": viol_cont, "viol_line": viol_line, "viol_scen": viol_scen, "rows_used": rows_used}


def reference(lodf, flow, out_flow, limits, ptdf_mon, ptdf_out, viol_cont, viol_line, viol_scen, rows_used):
    def screen(pair):
        lodf_block, flow_block = pair
        post = flow_block[:, :, None] + lodf_block.astype(jnp.float32)[:, None, :] * out_flow[None, :, :]
        return jnp.max(jnp.abs(post), axis=2)

    local = lax.map(screen, (lodf.reshape(L // 8, 8, K), flow.reshape(L // 8, 8, S))).reshape(L, S)
    worst = local / limits[:, None]

    def device_term(acc, device):
        cont_id = device // (N_LINE * N_SCEN)
        line_id = (device // N_SCEN) % N_LINE
        scen_id = device % N_SCEN
        start = device * ROWS_DEV
        cont_ids = lax.dynamic_slice_in_dim(viol_cont, start, ROWS_DEV) + cont_id * CONT_DEV
        line_ids = lax.dynamic_slice_in_dim(viol_line, start, ROWS_DEV) + line_id * LINE_DEV
        scen_ids = lax.dynamic_slice_in_dim(viol_scen, start, ROWS_DEV) + scen_id * SCEN_DEV
        coef = lodf[line_ids, cont_ids].astype(jnp.float32)
        rows = (ptdf_mon[line_ids].astype(jnp.float32) + coef[:, None] * ptdf_out[cont_ids].astype(jnp.float32)).astype(jnp.bfloat16)
        rows = lax.optimization_barrier(rows)
        post = flow[line_ids, scen_ids] + coef * out_flow[scen_ids, cont_ids]
        ratio = post / limits[line_ids]
        live = jnp.arange(ROWS_DEV, dtype=jnp.int32) < lax.dynamic_index_in_dim(rows_used, device, 0, keepdims=False)
        weight = jnp.where(live, 1.0 + ratio * ratio, jnp.zeros_like(ratio))
        wide = rows.astype(jnp.float32)
        scaled = (weight[:, None] * wide).astype(jnp.bfloat16)
        scaled = lax.optimization_barrier(scaled).astype(jnp.float32)
        term = jnp.dot(wide.T, scaled, precision=lax.Precision.HIGHEST, preferred_element_type=jnp.float32)
        return acc + term, None

    total, unused = lax.scan(device_term, jnp.zeros((G, G), jnp.float32), jnp.arange(DEVICES, dtype=jnp.int32))
    schur = total * (1.0 / (ROWS_DEV * DEVICES))
    return worst, schur
```

```python
import functools
import math

import jax
import jax.numpy as jnp
from jax import lax
from jax.experimental import pallas as pl
from jax.experimental.pallas import tpu as pltpu
from jax.sharding import PartitionSpec as P


MESH = pl.DeviceIdType.MESH
F32 = jnp.float32
BF16 = jnp.bfloat16
CODE = 32767.0


def encode(x):
    top = jnp.maximum(jnp.max(jnp.abs(x)), 1e-30)
    unit = x * (1.0 / top)
    root = unit * lax.rsqrt(jnp.maximum(jnp.abs(unit), 1e-30)) * CODE
    code = jnp.clip(jnp.round(root), -CODE, CODE).astype(jnp.int32).astype(jnp.int16)
    return code, jnp.full((8, 128), top * (1.0 / (CODE * CODE)), F32)


def decode(code, unit):
    root = code.astype(jnp.int32).astype(F32)
    return root * jnp.abs(root) * unit[0:1, 0:1]


def kernel(
    dims, meta_ref, lim_ref, lodf_ref, flow_ref, out_flow_ref, mon_ref, out_ref,
    worst_ref, schur_ref,
    meta, lodf32, flow_t, high, low, loading, pick, weight, left, scaled, own,
    q_send, q_recv, u_send, u_recv, meta_ss, meta_rs, load_ss, load_rs, send_sems, recv_sems,
):
    n_cont, n_scen, devices = dims
    c, m, q = lax.axis_index("cont"), lax.axis_index("line"), lax.axis_index("scen")
    pair = c + 1 - 2 * lax.rem(c, 2)
    middle = n_cont - 1 - c
    outer = jnp.logical_or(c == 0, c == n_cont - 1)
    inner = jnp.logical_not(outer)
    other = 1 - m
    n_rows = meta_ref.shape[1]
    lines, width = mon_ref.shape
    conts = out_ref.shape[0]
    scens = flow_ref.shape[1]
    block = schur_ref.shape[0]
    chunks = width // block
    parts = n_rows // 128

    barrier = pltpu.get_barrier_semaphore()
    for d in range(1, n_scen):
        pl.semaphore_signal(barrier, inc=1, device_id={"scen": lax.rem(q + d, n_scen)}, device_id_type=MESH)
    for d in range(1, n_cont):
        pl.semaphore_signal(barrier, inc=1, device_id={"cont": lax.rem(c + d, n_cont)}, device_id_type=MESH)
    pl.semaphore_signal(barrier, inc=1, device_id={"line": other}, device_id_type=MESH)

    meta[8 * n_scen:, :] = jnp.zeros((128 - 8 * n_scen, n_rows), F32)
    for p in range(parts):
        at = slice(p * 128, (p + 1) * 128)
        cols = jnp.transpose(jnp.concatenate([meta_ref[:, at], jnp.zeros((120, 128), F32)], axis=0))
        v_line, v_cont, v_scen, used = cols[:, 0:1], cols[:, 1:2], cols[:, 2:3], cols[:, 3:4]
        lane = lax.broadcasted_iota(jnp.int32, (128, 128), 1)
        is_line = lax.broadcasted_iota(jnp.int32, (128, lines), 1).astype(F32) == v_line
        is_cont = lax.broadcasted_iota(jnp.int32, (128, conts), 1).astype(F32) == v_cont
        is_scen = lax.broadcasted_iota(jnp.int32, (128, scens), 1).astype(F32) == v_scen
        one_line, one_scen = is_line.astype(F32), is_scen.astype(F32)
        row = jnp.dot(one_line.astype(BF16), lodf_ref[...], preferred_element_type=F32)
        coef = jnp.sum(jnp.where(is_cont, row, 0.0), axis=1, keepdims=True)
        row = jnp.dot(one_line, flow_ref[...], precision=lax.Precision.HIGHEST, preferred_element_type=F32)
        base = jnp.sum(jnp.where(is_scen, row, 0.0), axis=1, keepdims=True)
        row = jnp.dot(one_scen, out_flow_ref[...], precision=lax.Precision.HIGHEST, preferred_element_type=F32)
        outage = jnp.sum(jnp.where(is_cont, row, 0.0), axis=1, keepdims=True)
        limit = jnp.sum(jnp.where(is_line, lim_ref[...], 0.0), axis=1, keepdims=True)
        ratio = (base + coef * outage) / limit
        place = lax.broadcasted_iota(jnp.int32, (128, 1), 0).astype(F32) + float(p * 128)
        w = jnp.where(place < used, 1.0 + ratio * ratio, 0.0)
        facts = jnp.where(lane == 0, v_line, jnp.where(lane == 1, v_cont, jnp.where(lane == 2, coef, jnp.where(lane == 3, w, 0.0))))
        meta[pl.ds(pl.multiple_of(q * 8, 8), 8), at] = jnp.transpose(facts)[0:8, :]

    def meta_copy(source, target):
        rows = meta.at[pl.ds(pl.multiple_of(source * 8, 8), 8), :]
        return pltpu.make_async_remote_copy(
            src_ref=rows, dst_ref=rows, send_sem=meta_ss.at[target], recv_sem=meta_rs.at[source],
            device_id={"scen": target}, device_id_type=MESH)

    pl.semaphore_wait(barrier, n_scen + n_cont - 1)
    for d in range(1, n_scen):
        meta_copy(q, lax.rem(q + d, n_scen)).start()

    lodf32[...] = lodf_ref[...].astype(F32)
    flow_t[...] = jnp.transpose(jnp.concatenate([flow_ref[...], jnp.zeros((lines, 128 - scens), F32)], axis=1))
    high[...] = jnp.zeros_like(high)
    low[...] = jnp.zeros_like(low)

    for d in range(1, n_scen):
        source = lax.rem(q + d, n_scen)
        meta_copy(source, source).wait_recv()

    for s in range(n_scen):
        for p in range(parts):
            facts = jnp.transpose(meta[:, p * 128:(p + 1) * 128])
            f = facts[:, s * 8:(s + 1) * 8]
            at = slice(s * n_rows + p * 128, s * n_rows + (p + 1) * 128)
            lane = lax.broadcasted_iota(jnp.int32, (128, lines), 1).astype(F32)
            pick[at, 0:lines] = jnp.where(lane == f[:, 0:1], 1.0, 0.0).astype(BF16)
            lane = lax.broadcasted_iota(jnp.int32, (128, conts), 1).astype(F32)
            pick[at, lines:] = jnp.where(lane == f[:, 1:2], f[:, 2:3], 0.0).astype(BF16)
            weight[at, :] = jnp.broadcast_to(f[:, 3:4], (128, 128))

    def rows_of(s, column):
        at = pl.ds(pl.multiple_of(s * n_rows, n_rows), n_rows)
        cols = pl.ds(pl.multiple_of(column, block), block)
        full = jnp.dot(pick[at, 0:lines], mon_ref[:, cols], preferred_element_type=F32)
        full = full + jnp.dot(pick[at, lines:], out_ref[:, cols], preferred_element_type=F32)
        return full.astype(BF16)

    def left_step(s, carry):
        at = pl.ds(pl.multiple_of(s * n_rows, n_rows), n_rows)
        left[0:block, at] = jnp.transpose(rows_of(s, (m * n_scen + q) * block).astype(F32)).astype(BF16)
        left[block:, at] = jnp.transpose(rows_of(s, (other * n_scen + q) * block).astype(F32)).astype(BF16)
        return carry

    lax.fori_loop(0, n_scen, left_step, 0)

    def link(stage, j, to):
        kinds = ((q_send, q_recv), (u_send, u_recv))
        return [
            pltpu.make_async_remote_copy(
                src_ref=a.at[stage, j], dst_ref=b.at[stage, j], send_sem=send_sems.at[kind, stage, j],
                recv_sem=recv_sems.at[kind, stage, j], device_id=to, device_id_type=MESH)
            for kind, (a, b) in enumerate(kinds)
        ]

    to_line, to_pair, to_middle = {"line": other}, {"cont": pair}, {"cont": middle}

    def send(stage, j, to, value):
        code, unit = encode(value)
        q_send[stage, j] = code
        u_send[stage, j] = unit
        for copy in link(stage, j, to):
            copy.start()

    def received(stage, j, to):
        for copy in link(stage, j, to):
            copy.wait_recv()
        return decode(q_recv[stage, j], u_recv[stage, j])

    def put(j, value):
        schur_ref[:, pl.ds(pl.multiple_of(j * block, block), block)] = value * (1.0 / (n_rows * devices))

    def load_copy(source, target):
        return pltpu.make_async_remote_copy(
            src_ref=loading.at[source], dst_ref=loading.at[source], send_sem=load_ss.at[target],
            recv_sem=load_rs.at[source], device_id={"cont": target}, device_id_type=MESH)

    lines_each = lines // chunks

    def screen_line(line, carry):
        factors = lodf32[pl.ds(line, 1), :]
        tall = short = None
        for k in range(conts // 128):
            move = out_flow_ref[:, k * 128:(k + 1) * 128] * factors[:, k * 128:(k + 1) * 128]
            tall = move if tall is None else jnp.maximum(tall, move)
            short = move if short is None else jnp.minimum(short, move)
        here = lax.broadcasted_iota(jnp.int32, (scens, lines), 1) == line
        high[...] = jnp.where(here, jnp.max(tall, axis=1, keepdims=True), high[...])
        low[...] = jnp.where(here, jnp.min(short, axis=1, keepdims=True), low[...])
        return carry

    def turn(t, carry):
        @pl.when(t < chunks)
        def _():
            def scale_step(s, inside):
                at = pl.ds(pl.multiple_of(s * n_rows, n_rows), n_rows)
                w = weight[at, :]
                w = jnp.concatenate([w] * (block // 128), axis=1)
                scaled[at, :] = (rows_of(s, t * block).astype(F32) * w).astype(BF16)
                return inside

            lax.fori_loop(0, n_scen, scale_step, 0)
            send(0, t, to_line, jnp.dot(left[block:, :], scaled[...], preferred_element_type=F32))
            own[t] = jnp.dot(left[0:block, :], scaled[...], preferred_element_type=F32)
            lax.fori_loop(t * lines_each, (t + 1) * lines_each, screen_line, 0)

        @pl.when(jnp.logical_and(outer, t >= 4))
        def _():
            put(t - 4, received(3, t - 4, to_pair))

        @pl.when(jnp.logical_and(inner, jnp.logical_and(t >= 3, t < chunks + 3)))
        def _():
            j = t - 3
            far = received(2, j, to_middle)
            send(3, j, to_pair, decode(q_send[2, j], u_send[2, j]) + far)
            put(j, decode(q_send[3, j], u_send[3, j]))

        @pl.when(jnp.logical_and(inner, jnp.logical_and(t >= 2, t < chunks + 2)))
        def _():
            send(2, t - 2, to_middle, own[t - 2] + received(1, t - 2, to_pair))

        @pl.when(jnp.logical_and(t >= 1, t < chunks + 1))
        def _():
            total = own[t - 1] + received(0, t - 1, to_line)

            @pl.when(outer)
            def _():
                send(1, t - 1, to_pair, total)

            @pl.when(inner)
            def _():
                own[t - 1] = total

        @pl.when(t == chunks)
        def _():
            loading[c] = jnp.maximum(jnp.abs(flow_t[0:scens, :] + high[...]), jnp.abs(flow_t[0:scens, :] + low[...]))
            for d in range(1, n_cont):
                load_copy(c, lax.rem(c + d, n_cont)).start()

        return carry

    lax.fori_loop(0, chunks + 4, turn, 0)

    for d in range(1, n_cont):
        source = lax.rem(c + d, n_cont)
        load_copy(source, source).wait_recv()
    top = loading[0]
    for k in range(1, n_cont):
        top = jnp.maximum(top, loading[k])
    top = top / lim_ref[...]
    worst_ref[...] = jnp.transpose(jnp.concatenate([top, jnp.zeros((128 - scens, lines), F32)], axis=0))[:, 0:scens]

    for d in range(1, n_scen):
        meta_copy(q, lax.rem(q + d, n_scen)).wait_send()
    for d in range(1, n_cont):
        load_copy(c, lax.rem(c + d, n_cont)).wait_send()

    def drain(j, carry):
        for copy in link(0, j, to_line):
            copy.wait_send()

        @pl.when(outer)
        def _():
            for copy in link(1, j, to_pair):
                copy.wait_send()

        @pl.when(inner)
        def _():
            for copy in link(2, j, to_middle) + link(3, j, to_pair):
                copy.wait_send()

        return carry

    lax.fori_loop(0, chunks, drain, 0)


def fused(lodf, flow, out_flow, limits, ptdf_mon, ptdf_out, viol_cont, viol_line, viol_scen, rows_used):
    lines, conts = lodf.shape
    scens = flow.shape[1]
    width = ptdf_mon.shape[1]
    n_rows = viol_cont.shape[0]
    n_cont, n_line, n_scen = lax.axis_size("cont"), lax.axis_size("line"), lax.axis_size("scen")
    block = width // (n_line * n_scen)
    chunks = width // block
    used = jnp.broadcast_to(rows_used.astype(F32), (n_rows,))
    zero = jnp.zeros((n_rows,), F32)
    meta = jnp.stack([viol_line.astype(F32), viol_cont.astype(F32), viol_scen.astype(F32), used, zero, zero, zero, zero])
    listed = n_scen * n_rows
    vmem = pl.BlockSpec(memory_space=pltpu.VMEM)
    dma = pltpu.SemaphoreType.DMA
    return pl.pallas_call(
        functools.partial(kernel, (n_cont, n_scen, n_cont * n_line * n_scen)),
        out_shape=(jax.ShapeDtypeStruct((lines, scens), F32), jax.ShapeDtypeStruct((block, width), F32)),
        in_specs=[vmem] * 7,
        out_specs=(vmem, vmem),
        scratch_shapes=[
            pltpu.VMEM((128, n_rows), F32),
            pltpu.VMEM((lines, conts), F32),
            pltpu.VMEM((128, lines), F32),
            pltpu.VMEM((scens, lines), F32),
            pltpu.VMEM((scens, lines), F32),
            pltpu.VMEM((n_cont, scens, lines), F32),
            pltpu.VMEM((listed, lines + conts), BF16),
            pltpu.VMEM((listed, 128), F32),
            pltpu.VMEM((2 * block, listed), BF16),
            pltpu.VMEM((listed, block), BF16),
            pltpu.VMEM((chunks, block, block), F32),
            pltpu.VMEM((4, chunks, block, block), jnp.int16),
            pltpu.VMEM((4, chunks, block, block), jnp.int16),
            pltpu.VMEM((4, chunks, 8, 128), F32),
            pltpu.VMEM((4, chunks, 8, 128), F32),
            dma((n_scen,)), dma((n_scen,)), dma((n_cont,)), dma((n_cont,)),
            dma((2, 4, chunks)), dma((2, 4, chunks)),
        ],
        compiler_params=pltpu.CompilerParams(collective_id=0, has_side_effects=True, vmem_limit_bytes=56 * 1024 * 1024),
    )(meta, limits.reshape(1, lines), lodf, flow, out_flow, ptdf_mon, ptdf_out)


def local(
    lodf, flow, out_flow, limits, ptdf_mon, ptdf_out, viol_cont, viol_line, viol_scen, rows_used
):
    line_dev, cont_dev = lodf.shape
    scen_dev = flow.shape[1]
    width = ptdf_mon.shape[1]
    n_rows = viol_cont.shape[0]
    block = width // (lax.axis_size("line") * lax.axis_size("scen"))
    if (
        (lax.axis_size("cont"), lax.axis_size("line")) == (4, 2)
        and line_dev == 128 and scen_dev <= 128 and scen_dev % 8 == 0
        and block % 256 == 0 and n_rows % 128 == 0 and cont_dev % 128 == 0
    ):
        return fused(
            lodf, flow, out_flow, limits, ptdf_mon, ptdf_out, viol_cont, viol_line, viol_scen, rows_used
        )
    n_cont = lax.axis_size("cont")
    n_line = lax.axis_size("line")
    n_scen = lax.axis_size("scen")
    owners = n_line * n_scen
    devices = n_cont * owners
    row_block = math.gcd(n_rows, 512)
    lines_each = math.gcd(line_dev, 32)

    def screen(pair):
        lodf_block, flow_block = pair
        post = (
            flow_block[:, :, None]
            + lodf_block.astype(jnp.float32)[:, None, :] * out_flow[None, :, :]
        )
        return jnp.max(jnp.abs(post), axis=2)

    local_worst = lax.map(
        screen,
        (
            lodf.reshape(line_dev // lines_each, lines_each, cont_dev),
            flow.reshape(line_dev // lines_each, lines_each, scen_dev),
        ),
    ).reshape(line_dev, scen_dev)
    worst = lax.pmax(local_worst, "cont") / limits[:, None]
    coef = lodf[viol_line, viol_cont].astype(jnp.float32)
    rows = (
        ptdf_mon[viol_line].astype(jnp.float32)
        + coef[:, None] * ptdf_out[viol_cont].astype(jnp.float32)
    ).astype(jnp.bfloat16)
    rows = lax.optimization_barrier(rows)
    post = flow[viol_line, viol_scen] + coef * out_flow[viol_scen, viol_cont]
    ratio = post / limits[viol_line]
    live = jnp.arange(n_rows, dtype=jnp.int32) < rows_used[0]
    weight = jnp.where(live, 1.0 + ratio * ratio, jnp.zeros_like(ratio))
    scaled = (weight[:, None] * rows.astype(jnp.float32)).astype(jnp.bfloat16)
    trips = (rows_used[0] + row_block - 1) // row_block
    row_blocks = rows.reshape(n_rows // row_block, row_block, width)
    scaled_blocks = scaled.reshape(n_rows // row_block, row_block, width)

    def step(index, acc):
        row_tile = lax.dynamic_index_in_dim(row_blocks, index, 0, keepdims=False)
        scaled_tile = lax.dynamic_index_in_dim(scaled_blocks, index, 0, keepdims=False)
        return acc + lax.dot_general(
            row_tile, scaled_tile, (((0,), (0,)), ((), ())), preferred_element_type=jnp.float32
        )

    owned = lax.psum_scatter(
        lax.fori_loop(
            0,
            trips,
            step,
            jnp.zeros((lax.axis_size(("line", "scen")) * (width // owners), width), jnp.float32),
        ),
        ("line", "scen"),
        scatter_dimension=0,
        tiled=True,
    )
    total = lax.psum(owned, "cont")
    schur = total * (1.0 / (n_rows * devices))
    return (worst, schur)


def solution(mesh):
    in_specs = (
        P("line", "cont"),
        P("line", "scen"),
        P("scen", "cont"),
        P("line"),
        P("line", None),
        P("cont", None),
        P(("cont", "line", "scen")),
        P(("cont", "line", "scen")),
        P(("cont", "line", "scen")),
        P(("cont", "line", "scen")),
    )
    out_specs = (P("line", "scen"), P(("line", "scen"), None))
    return jax.shard_map(local, mesh=mesh, in_specs=in_specs, out_specs=out_specs, check_vma=False)
```

```python
import functools
import math

import jax
import jax.numpy as jnp
from jax import lax
from jax.experimental import pallas as pl
from jax.experimental.pallas import tpu as pltpu
from jax.sharding import PartitionSpec as P


MESH = pl.DeviceIdType.MESH
F32 = jnp.float32
BF16 = jnp.bfloat16
CODE = 32760.0


def encode(x):
    top = jnp.maximum(jnp.max(jnp.abs(x), axis=0, keepdims=True), 1e-30)
    unit = x * (1.0 / top)
    root = unit * lax.rsqrt(jnp.maximum(jnp.abs(unit), 1e-30)) * CODE
    code = jnp.round(root).astype(jnp.int32).astype(jnp.int16)
    return code, jnp.broadcast_to(top * (1.0 / (CODE * CODE)), (8, x.shape[1]))


def decode(code, unit):
    root = code.astype(jnp.int32).astype(F32)
    return root * jnp.abs(root) * unit[0:1, :]


def kernel(
    dims, line_ref, cont_ref, scen_ref, used_ref, lim_ref, lodf_ref, flow_t, out_flow_ref, mon_ref, out_ref,
    worst_ref, code_ref, unit_ref,
    meta, lodf32, high, low, loading, pick, weight, left, scaled, own,
    q_send, q_recv, u_send, u_recv, meta_ss, meta_rs, load_ss, load_rs, send_sems, recv_sems,
):
    n_cont, n_line, n_scen = dims
    c, m, q = lax.axis_index("cont"), lax.axis_index("line"), lax.axis_index("scen")
    pair = c + 1 - 2 * lax.rem(c, 2)
    middle = n_cont - 1 - c
    outer = jnp.logical_or(c == 0, c == n_cont - 1)
    inner = jnp.logical_not(outer)
    other = 1 - m
    n_rows = line_ref.shape[1]
    lines, width = mon_ref.shape
    conts = out_ref.shape[0]
    scens = flow_t.shape[0]
    block = code_ref.shape[0]
    chunks = width // block
    half = block // 2
    items = 2 * chunks
    parts = n_rows // 128

    barrier = pltpu.get_barrier_semaphore()
    for d in range(1, n_scen):
        pl.semaphore_signal(barrier, inc=1, device_id={"scen": lax.rem(q + d, n_scen)}, device_id_type=MESH)
    for d in range(1, n_cont):
        pl.semaphore_signal(barrier, inc=1, device_id={"cont": lax.rem(c + d, n_cont)}, device_id_type=MESH)
    pl.semaphore_signal(barrier, inc=1, device_id={"line": other}, device_id_type=MESH)

    meta[8 * n_scen:, :] = jnp.zeros((128 - 8 * n_scen, n_rows), F32)
    for p in range(parts):
        at = slice(p * 128, (p + 1) * 128)
        sub = lax.broadcasted_iota(jnp.int32, (128, 128), 0)
        cols = jnp.where(sub == 0, line_ref[:, at], jnp.where(sub == 1, cont_ref[:, at], jnp.where(sub == 2, scen_ref[:, at], used_ref[...])))
        cols = jnp.transpose(cols.astype(F32))
        v_line, v_cont, v_scen, used = cols[:, 0:1], cols[:, 1:2], cols[:, 2:3], cols[:, 3:4]
        lane = lax.broadcasted_iota(jnp.int32, (128, 128), 1)
        is_line = lax.broadcasted_iota(jnp.int32, (128, lines), 1).astype(F32) == v_line
        is_cont = lax.broadcasted_iota(jnp.int32, (128, conts), 1).astype(F32) == v_cont
        is_scen = lax.broadcasted_iota(jnp.int32, (128, scens), 1).astype(F32) == v_scen
        one_line, one_scen = is_line.astype(F32), is_scen.astype(F32)
        row = jnp.dot(one_line.astype(BF16), lodf_ref[...], preferred_element_type=F32)
        coef = jnp.sum(jnp.where(is_cont, row, 0.0), axis=1, keepdims=True)
        row = jnp.dot(one_scen, flow_t[...], precision=lax.Precision.HIGHEST, preferred_element_type=F32)
        base = jnp.sum(jnp.where(is_line, row, 0.0), axis=1, keepdims=True)
        row = jnp.dot(one_scen, out_flow_ref[...], precision=lax.Precision.HIGHEST, preferred_element_type=F32)
        outage = jnp.sum(jnp.where(is_cont, row, 0.0), axis=1, keepdims=True)
        limit = jnp.sum(jnp.where(is_line, lim_ref[...], 0.0), axis=1, keepdims=True)
        ratio = (base + coef * outage) / limit
        place = lax.broadcasted_iota(jnp.int32, (128, 1), 0).astype(F32) + float(p * 128)
        w = jnp.where(place < used, 1.0 + ratio * ratio, 0.0)
        facts = jnp.where(lane == 0, v_line, jnp.where(lane == 1, v_cont, jnp.where(lane == 2, coef, jnp.where(lane == 3, w, 0.0))))
        meta[pl.ds(pl.multiple_of(q * 8, 8), 8), at] = jnp.transpose(facts)[0:8, :]

    def meta_copy(source, target):
        rows = meta.at[pl.ds(pl.multiple_of(source * 8, 8), 8), :]
        return pltpu.make_async_remote_copy(
            src_ref=rows, dst_ref=rows, send_sem=meta_ss.at[target], recv_sem=meta_rs.at[source],
            device_id={"scen": target}, device_id_type=MESH)

    pl.semaphore_wait(barrier, n_scen + n_cont - 1)
    for d in range(1, n_scen):
        meta_copy(q, lax.rem(q + d, n_scen)).start()

    lodf32[...] = lodf_ref[...].astype(F32)
    high[...] = jnp.zeros_like(high)
    low[...] = jnp.zeros_like(low)

    for d in range(1, n_scen):
        source = lax.rem(q + d, n_scen)
        meta_copy(source, source).wait_recv()

    for s in range(n_scen):
        for p in range(parts):
            facts = jnp.transpose(meta[:, p * 128:(p + 1) * 128])
            f = facts[:, s * 8:(s + 1) * 8]
            at = slice(s * n_rows + p * 128, s * n_rows + (p + 1) * 128)
            lane = lax.broadcasted_iota(jnp.int32, (128, lines), 1).astype(F32)
            pick[at, 0:lines] = jnp.where(lane == f[:, 0:1], 1.0, 0.0).astype(BF16)
            lane = lax.broadcasted_iota(jnp.int32, (128, conts), 1).astype(F32)
            pick[at, lines:] = jnp.where(lane == f[:, 1:2], f[:, 2:3], 0.0).astype(BF16)
            weight[at, :] = jnp.broadcast_to(f[:, 3:4], (128, 128))

    def rows_of(s, column):
        at = pl.ds(pl.multiple_of(s * n_rows, n_rows), n_rows)
        cols = pl.ds(pl.multiple_of(column, block), block)
        full = jnp.dot(pick[at, 0:lines], mon_ref[:, cols], preferred_element_type=F32)
        full = full + jnp.dot(pick[at, lines:], out_ref[:, cols], preferred_element_type=F32)
        return full.astype(BF16)

    def screen(first, count):
        top, bottom = high[...], low[...]
        place = lax.broadcasted_iota(jnp.int32, (scens, lines), 1)
        for i in range(count):
            factors = lodf32[pl.ds(first + i, 1), :]
            tall = short = None
            for k in range(conts // 128):
                move = out_flow_ref[:, k * 128:(k + 1) * 128] * factors[:, k * 128:(k + 1) * 128]
                tall = move if tall is None else jnp.maximum(tall, move)
                short = move if short is None else jnp.minimum(short, move)
            top = jnp.where(place == first + i, jnp.max(tall, axis=1, keepdims=True), top)
            bottom = jnp.where(place == first + i, jnp.min(short, axis=1, keepdims=True), bottom)
        high[...] = top
        low[...] = bottom

    lines_each = lines // (chunks * n_scen)

    def scale(s, slot, rows):
        at = pl.ds(pl.multiple_of(s * n_rows, n_rows), n_rows)
        w = weight[at, :]
        w = jnp.concatenate([w] * (block // 128), axis=1)
        scaled[slot, at, :] = (rows.astype(F32) * w).astype(BF16)

    def column(t):
        return (lax.rem(t, n_line) * n_scen + lax.rem(q + t // n_line, n_scen)) * block

    def left_step(s, carry):
        at = pl.ds(pl.multiple_of(s * n_rows, n_rows), n_rows)
        for line in range(n_line):
            rows = rows_of(s, column(line))
            left[line * block:(line + 1) * block, at] = jnp.transpose(rows.astype(F32)).astype(BF16)
            scale(s, line, rows)
        screen(s * n_line * lines_each, n_line * lines_each)
        return carry

    lax.fori_loop(0, n_scen, left_step, 0)

    def link(stage, j, to):
        kinds = ((q_send, q_recv), (u_send, u_recv))
        return [
            pltpu.make_async_remote_copy(
                src_ref=a.at[stage, j], dst_ref=b.at[stage, j], send_sem=send_sems.at[kind, stage, j],
                recv_sem=recv_sems.at[kind, stage, j], device_id=to, device_id_type=MESH)
            for kind, (a, b) in enumerate(kinds)
        ]

    to_line, to_pair, to_middle = {"line": other}, {"cont": pair}, {"cont": middle}

    def send(stage, j, to, value):
        code, unit = encode(value)
        q_send[stage, j] = code
        u_send[stage, j] = unit
        for copy in link(stage, j, to):
            copy.start()

    def received(stage, j, to):
        for copy in link(stage, j, to):
            copy.wait_recv()
        return decode(q_recv[stage, j], u_recv[stage, j])

    def put(i, code, unit):
        at = pl.ds(pl.multiple_of(lax.rem(i, 2) * half, half), half)
        cols = pl.ds(pl.multiple_of(column(i // 2), block), block)
        code_ref[at, cols] = code
        unit_ref[pl.ds(pl.multiple_of(lax.rem(i, 2) * 8, 8), 8), cols] = unit

    def mine(i):
        return own.at[i // 2, pl.ds(pl.multiple_of(m * block + lax.rem(i, 2) * half, half), half), :]

    def load_copy(source, target):
        return pltpu.make_async_remote_copy(
            src_ref=loading.at[source], dst_ref=loading.at[source], send_sem=load_ss.at[target],
            recv_sem=load_rs.at[source], device_id={"cont": target}, device_id_type=MESH)

    def turn(u, carry):
        @pl.when(jnp.logical_and(lax.rem(u, 2) == 0, u < items))
        def _():
            t = u // 2
            slot = lax.rem(t, n_line)

            @pl.when(t >= n_line)
            def _():
                def scale_step(s, inside):
                    scale(s, slot, rows_of(s, column(t)))
                    screen((t * n_scen + s) * lines_each, lines_each)
                    return inside

                lax.fori_loop(0, n_scen, scale_step, 0)

            own[t] = jnp.dot(left[...], scaled[slot], preferred_element_type=F32)
            for h in range(2):
                send(0, u + h, to_line, own[t, pl.ds(pl.multiple_of(other * block + h * half, half), half), :])

        @pl.when(jnp.logical_and(outer, u >= 8))
        def _():
            i = u - 8
            for copy in link(3, i, to_pair):
                copy.wait_recv()
            put(i, q_recv[3, i], u_recv[3, i])

        @pl.when(jnp.logical_and(inner, jnp.logical_and(u >= 6, u < items + 6)))
        def _():
            i = u - 6
            far = received(2, i, to_middle)
            send(3, i, to_pair, decode(q_send[2, i], u_send[2, i]) + far)
            put(i, q_send[3, i], u_send[3, i])

        @pl.when(jnp.logical_and(inner, jnp.logical_and(u >= 4, u < items + 4)))
        def _():
            send(2, u - 4, to_middle, mine(u - 4)[...] + received(1, u - 4, to_pair))

        @pl.when(jnp.logical_and(u >= 2, u < items + 2))
        def _():
            total = mine(u - 2)[...] + received(0, u - 2, to_line)

            @pl.when(outer)
            def _():
                send(1, u - 2, to_pair, total)

            @pl.when(inner)
            def _():
                mine(u - 2)[...] = total

        @pl.when(u == items)
        def _():
            loading[c] = jnp.maximum(jnp.abs(flow_t[...] + high[...]), jnp.abs(flow_t[...] + low[...]))
            for d in range(1, n_cont):
                load_copy(c, lax.rem(c + d, n_cont)).start()

        return carry

    lax.fori_loop(0, items + 8, turn, 0)

    for d in range(1, n_cont):
        source = lax.rem(c + d, n_cont)
        load_copy(source, source).wait_recv()
    top = loading[0]
    for k in range(1, n_cont):
        top = jnp.maximum(top, loading[k])
    worst_ref[...] = top / lim_ref[...]

    for d in range(1, n_scen):
        meta_copy(q, lax.rem(q + d, n_scen)).wait_send()
    for d in range(1, n_cont):
        load_copy(c, lax.rem(c + d, n_cont)).wait_send()

    def drain(j, carry):
        for copy in link(0, j, to_line):
            copy.wait_send()

        @pl.when(outer)
        def _():
            for copy in link(1, j, to_pair):
                copy.wait_send()

        @pl.when(inner)
        def _():
            for copy in link(2, j, to_middle) + link(3, j, to_pair):
                copy.wait_send()

        return carry

    lax.fori_loop(0, items, drain, 0)


def fused(lodf, flow, out_flow, limits, ptdf_mon, ptdf_out, viol_cont, viol_line, viol_scen, rows_used):
    lines, conts = lodf.shape
    scens = flow.shape[1]
    width = ptdf_mon.shape[1]
    n_rows = viol_cont.shape[0]
    n_cont, n_line, n_scen = lax.axis_size("cont"), lax.axis_size("line"), lax.axis_size("scen")
    block = width // (n_line * n_scen)
    chunks = width // block
    half = block // 2
    items = 2 * chunks
    listed = n_scen * n_rows
    vmem = pl.BlockSpec(memory_space=pltpu.VMEM)
    dma = pltpu.SemaphoreType.DMA
    worst_t, code, unit = pl.pallas_call(
        functools.partial(kernel, (n_cont, n_line, n_scen)),
        out_shape=(
            jax.ShapeDtypeStruct((scens, lines), F32),
            jax.ShapeDtypeStruct((block, width), jnp.int16),
            jax.ShapeDtypeStruct((16, width), F32),
        ),
        in_specs=[vmem] * 10,
        out_specs=(vmem, vmem, vmem),
        scratch_shapes=[
            pltpu.VMEM((128, n_rows), F32),
            pltpu.VMEM((lines, conts), F32),
            pltpu.VMEM((scens, lines), F32),
            pltpu.VMEM((scens, lines), F32),
            pltpu.VMEM((n_cont, scens, lines), F32),
            pltpu.VMEM((listed, lines + conts), BF16),
            pltpu.VMEM((listed, 128), F32),
            pltpu.VMEM((2 * block, listed), BF16),
            pltpu.VMEM((n_line, listed, block), BF16),
            pltpu.VMEM((chunks, n_line * block, block), F32),
            pltpu.VMEM((4, items, half, block), jnp.int16),
            pltpu.VMEM((4, items, half, block), jnp.int16),
            pltpu.VMEM((4, items, 8, block), F32),
            pltpu.VMEM((4, items, 8, block), F32),
            dma((n_scen,)), dma((n_scen,)), dma((n_cont,)), dma((n_cont,)),
            dma((2, 4, items)), dma((2, 4, items)),
        ],
        compiler_params=pltpu.CompilerParams(collective_id=0, has_side_effects=True, vmem_limit_bytes=56 * 1024 * 1024),
    )(
        viol_line.reshape(1, n_rows), viol_cont.reshape(1, n_rows), viol_scen.reshape(1, n_rows),
        jnp.broadcast_to(rows_used, (1, 128)), limits.reshape(1, lines), lodf, flow.T, out_flow, ptdf_mon, ptdf_out,
    )
    root = code.astype(F32).reshape(2, half, width)
    unit = unit.reshape(2, 8, width)[:, 0:1, :] * (1.0 / (n_rows * n_cont * n_line * n_scen))
    return worst_t.T, (root * jnp.abs(root) * unit).reshape(block, width)


def local(
    lodf, flow, out_flow, limits, ptdf_mon, ptdf_out, viol_cont, viol_line, viol_scen, rows_used
):
    line_dev, cont_dev = lodf.shape
    scen_dev = flow.shape[1]
    width = ptdf_mon.shape[1]
    n_rows = viol_cont.shape[0]
    block = width // (lax.axis_size("line") * lax.axis_size("scen"))
    if (
        (lax.axis_size("cont"), lax.axis_size("line"), lax.axis_size("scen")) == (4, 2, 4)
        and line_dev == 128 and scen_dev <= 128 and scen_dev % 8 == 0
        and block % 256 == 0 and n_rows % 128 == 0 and cont_dev % 128 == 0
    ):
        return fused(
            lodf, flow, out_flow, limits, ptdf_mon, ptdf_out, viol_cont, viol_line, viol_scen, rows_used
        )
    n_cont = lax.axis_size("cont")
    n_line = lax.axis_size("line")
    n_scen = lax.axis_size("scen")
    owners = n_line * n_scen
    devices = n_cont * owners
    row_block = math.gcd(n_rows, 512)
    lines_each = math.gcd(line_dev, 32)

    def screen(pair):
        lodf_block, flow_block = pair
        post = (
            flow_block[:, :, None]
            + lodf_block.astype(jnp.float32)[:, None, :] * out_flow[None, :, :]
        )
        return jnp.max(jnp.abs(post), axis=2)

    local_worst = lax.map(
        screen,
        (
            lodf.reshape(line_dev // lines_each, lines_each, cont_dev),
            flow.reshape(line_dev // lines_each, lines_each, scen_dev),
        ),
    ).reshape(line_dev, scen_dev)
    worst = lax.pmax(local_worst, "cont") / limits[:, None]
    coef = lodf[viol_line, viol_cont].astype(jnp.float32)
    rows = (
        ptdf_mon[viol_line].astype(jnp.float32)
        + coef[:, None] * ptdf_out[viol_cont].astype(jnp.float32)
    ).astype(jnp.bfloat16)
    rows = lax.optimization_barrier(rows)
    post = flow[viol_line, viol_scen] + coef * out_flow[viol_scen, viol_cont]
    ratio = post / limits[viol_line]
    live = jnp.arange(n_rows, dtype=jnp.int32) < rows_used[0]
    weight = jnp.where(live, 1.0 + ratio * ratio, jnp.zeros_like(ratio))
    scaled = (weight[:, None] * rows.astype(jnp.float32)).astype(jnp.bfloat16)
    trips = (rows_used[0] + row_block - 1) // row_block
    row_blocks = rows.reshape(n_rows // row_block, row_block, width)
    scaled_blocks = scaled.reshape(n_rows // row_block, row_block, width)

    def step(index, acc):
        row_tile = lax.dynamic_index_in_dim(row_blocks, index, 0, keepdims=False)
        scaled_tile = lax.dynamic_index_in_dim(scaled_blocks, index, 0, keepdims=False)
        return acc + lax.dot_general(
            row_tile, scaled_tile, (((0,), (0,)), ((), ())), preferred_element_type=jnp.float32
        )

    owned = lax.psum_scatter(
        lax.fori_loop(
            0,
            trips,
            step,
            jnp.zeros((lax.axis_size(("line", "scen")) * (width // owners), width), jnp.float32),
        ),
        ("line", "scen"),
        scatter_dimension=0,
        tiled=True,
    )
    total = lax.psum(owned, "cont")
    schur = total * (1.0 / (n_rows * devices))
    return (worst, schur)


def solution(mesh):
    in_specs = (
        P("line", "cont"),
        P("line", "scen"),
        P("scen", "cont"),
        P("line"),
        P("line", None),
        P("cont", None),
        P(("cont", "line", "scen")),
        P(("cont", "line", "scen")),
        P(("cont", "line", "scen")),
        P(("cont", "line", "scen")),
    )
    out_specs = (P("line", "scen"), P(("line", "scen"), None))
    return jax.shard_map(local, mesh=mesh, in_specs=in_specs, out_specs=out_specs, check_vma=False)
```

```python
import functools
import math

import jax
import jax.numpy as jnp
from jax import lax
from jax.experimental import pallas as pl
from jax.experimental.pallas import tpu as pltpu
from jax.sharding import PartitionSpec as P


MESH = pl.DeviceIdType.MESH
F32 = jnp.float32
BF16 = jnp.bfloat16
CODE = 32760.0


def encode(x):
    top = jnp.maximum(jnp.max(jnp.abs(x), axis=0, keepdims=True), 1e-30)
    power = jnp.ceil(jnp.log2(top) + 1e-3)
    unit = x * jnp.exp2(-power)
    root = unit * lax.rsqrt(jnp.maximum(jnp.abs(unit), 1e-30)) * CODE
    code = jnp.round(root).astype(jnp.int32).astype(jnp.int16)
    power = jnp.broadcast_to(power, (16, x.shape[1])).astype(jnp.int32).astype(jnp.int16)
    return code, power


def decode(code, power, factor=1.0):
    root = code.astype(jnp.int32).astype(F32)
    unit = jnp.exp2(power.astype(jnp.int32).astype(F32)[0:1, :]) * (factor / (CODE * CODE))
    return root * jnp.abs(root) * unit


def finish(factor, worst_in, code_ref, power_ref, worst_ref, schur_ref):
    worst_ref[...] = worst_in[...]
    half = code_ref.shape[0] // 2
    for h in range(2):
        at = slice(h * half, (h + 1) * half)
        schur_ref[at, :] = decode(code_ref[at, :], power_ref[h * 16:(h + 1) * 16, :], factor)


def kernel(
    dims, line_ref, cont_ref, scen_ref, used_ref, lim_ref, lodf_ref, flow_t, out_flow_ref, mon_ref, out_ref,
    worst_ref, code_ref, power_ref,
    meta, lodf32, high, low, loading, pick, weight, left, scaled, own,
    q_send, q_recv, meta_ss, meta_rs, load_ss, load_rs, send_sems, recv_sems,
):
    n_cont, n_line, n_scen = dims
    c, m, q = lax.axis_index("cont"), lax.axis_index("line"), lax.axis_index("scen")
    pair = c + 1 - 2 * lax.rem(c, 2)
    middle = n_cont - 1 - c
    outer = jnp.logical_or(c == 0, c == n_cont - 1)
    inner = jnp.logical_not(outer)
    other = 1 - m
    n_rows = line_ref.shape[1]
    lines, width = mon_ref.shape
    conts = out_ref.shape[0]
    scens = flow_t.shape[0]
    block = code_ref.shape[0]
    chunks = width // block
    half = block // 2
    items = 2 * chunks
    parts = n_rows // 128

    barrier = pltpu.get_barrier_semaphore()
    for d in range(1, n_scen):
        pl.semaphore_signal(barrier, inc=1, device_id={"scen": lax.rem(q + d, n_scen)}, device_id_type=MESH)
    for d in range(1, n_cont):
        pl.semaphore_signal(barrier, inc=1, device_id={"cont": lax.rem(c + d, n_cont)}, device_id_type=MESH)
    pl.semaphore_signal(barrier, inc=1, device_id={"line": other}, device_id_type=MESH)

    for p in range(parts):
        at = slice(p * 128, (p + 1) * 128)
        sub = lax.broadcasted_iota(jnp.int32, (128, 128), 0)
        cols = jnp.where(sub == 0, line_ref[:, at], jnp.where(sub == 1, cont_ref[:, at], jnp.where(sub == 2, scen_ref[:, at], used_ref[0])))
        cols = jnp.transpose(cols.astype(F32))
        v_line, v_cont, v_scen, used = cols[:, 0:1], cols[:, 1:2], cols[:, 2:3], cols[:, 3:4]
        lane = lax.broadcasted_iota(jnp.int32, (128, 128), 1)
        is_line = lax.broadcasted_iota(jnp.int32, (128, lines), 1).astype(F32) == v_line
        is_cont = lax.broadcasted_iota(jnp.int32, (128, conts), 1).astype(F32) == v_cont
        is_scen = lax.broadcasted_iota(jnp.int32, (128, scens), 1).astype(F32) == v_scen
        one_line, one_scen = is_line.astype(F32), is_scen.astype(F32)
        row = jnp.dot(one_line.astype(BF16), lodf_ref[...], preferred_element_type=F32)
        coef = jnp.sum(jnp.where(is_cont, row, 0.0), axis=1, keepdims=True)
        row = jnp.dot(one_scen, flow_t[...], precision=lax.Precision.HIGHEST, preferred_element_type=F32)
        base = jnp.sum(jnp.where(is_line, row, 0.0), axis=1, keepdims=True)
        row = jnp.dot(one_scen, out_flow_ref[...], precision=lax.Precision.HIGHEST, preferred_element_type=F32)
        outage = jnp.sum(jnp.where(is_cont, row, 0.0), axis=1, keepdims=True)
        limit = jnp.sum(jnp.where(is_line, lim_ref[...], 0.0), axis=1, keepdims=True)
        ratio = (base + coef * outage) / limit
        place = lax.broadcasted_iota(jnp.int32, (128, 1), 0).astype(F32) + float(p * 128)
        w = jnp.where(place < used, 1.0 + ratio * ratio, 0.0)
        facts = jnp.where(lane == 0, v_line, jnp.where(lane == 1, v_cont, jnp.where(lane == 2, coef, jnp.where(lane == 3, w, 0.0))))
        meta[pl.ds(pl.multiple_of(q * 8, 8), 8), at] = jnp.transpose(facts)[0:8, :]

    def meta_copy(source, target):
        rows = meta.at[pl.ds(pl.multiple_of(source * 8, 8), 8), :]
        return pltpu.make_async_remote_copy(
            src_ref=rows, dst_ref=rows, send_sem=meta_ss.at[target], recv_sem=meta_rs.at[source],
            device_id={"scen": target}, device_id_type=MESH)

    pl.semaphore_wait(barrier, n_scen + n_cont - 1)
    for d in range(1, n_scen):
        meta_copy(q, lax.rem(q + d, n_scen)).start()

    lodf32[...] = lodf_ref[...].astype(F32)
    high[...] = jnp.zeros_like(high)
    low[...] = jnp.zeros_like(low)

    def pick_rows(s):
        for p in range(parts):
            facts = meta[pl.ds(pl.multiple_of(s * 8, 8), 8), p * 128:(p + 1) * 128]
            f = jnp.transpose(jnp.concatenate([facts, jnp.zeros((120, 128), F32)], axis=0))
            at = pl.ds(pl.multiple_of(s * n_rows + p * 128, 128), 128)
            lane = lax.broadcasted_iota(jnp.int32, (128, lines), 1).astype(F32)
            pick[at, 0:lines] = jnp.where(lane == f[:, 0:1], 1.0, 0.0).astype(BF16)
            lane = lax.broadcasted_iota(jnp.int32, (128, conts), 1).astype(F32)
            pick[at, lines:] = jnp.where(lane == f[:, 1:2], f[:, 2:3], 0.0).astype(BF16)
            weight[at, :] = jnp.broadcast_to(f[:, 3:4], (128, 128))

    def rows_of(s, column):
        at = pl.ds(pl.multiple_of(s * n_rows, n_rows), n_rows)
        cols = pl.ds(pl.multiple_of(column, block), block)
        full = jnp.dot(pick[at, 0:lines], mon_ref[:, cols], preferred_element_type=F32)
        full = full + jnp.dot(pick[at, lines:], out_ref[:, cols], preferred_element_type=F32)
        return full.astype(BF16)

    def screen(first, count):
        top, bottom = high[...], low[...]
        place = lax.broadcasted_iota(jnp.int32, (scens, lines), 1)
        for i in range(count):
            factors = lodf32[pl.ds(first + i, 1), :]
            tall = short = None
            for k in range(conts // 128):
                move = out_flow_ref[:, k * 128:(k + 1) * 128] * factors[:, k * 128:(k + 1) * 128]
                tall = move if tall is None else jnp.maximum(tall, move)
                short = move if short is None else jnp.minimum(short, move)
            top = jnp.where(place == first + i, jnp.max(tall, axis=1, keepdims=True), top)
            bottom = jnp.where(place == first + i, jnp.min(short, axis=1, keepdims=True), bottom)
        high[...] = top
        low[...] = bottom

    lines_each = lines // (chunks * n_scen)

    def scale(s, slot, rows):
        at = pl.ds(pl.multiple_of(s * n_rows, n_rows), n_rows)
        w = weight[at, :]
        w = jnp.concatenate([w] * (block // 128), axis=1)
        scaled[slot, at, :] = (rows.astype(F32) * w).astype(BF16)

    def column(t):
        return (lax.rem(t, n_line) * n_scen + lax.rem(q + t // n_line, n_scen)) * block

    def left_step(d, carry):
        s = lax.rem(q + d, n_scen)

        @pl.when(d > 0)
        def _():
            meta_copy(s, s).wait_recv()

        pick_rows(s)
        at = pl.ds(pl.multiple_of(s * n_rows, n_rows), n_rows)
        for line in range(n_line):
            rows = rows_of(s, column(line))
            left[line * block:(line + 1) * block, at] = jnp.transpose(rows.astype(F32)).astype(BF16)
            scale(s, line, rows)
        screen(s * n_line * lines_each, n_line * lines_each)
        return carry

    lax.fori_loop(0, n_scen, left_step, 0)

    def link(stage, i, to):
        return pltpu.make_async_remote_copy(
            src_ref=q_send.at[stage, i], dst_ref=q_recv.at[stage, i], send_sem=send_sems.at[stage, i],
            recv_sem=recv_sems.at[stage, i], device_id=to, device_id_type=MESH)

    to_line, to_pair, to_middle = {"line": other}, {"cont": pair}, {"cont": middle}

    def send(stage, i, to, value):
        code, power = encode(value)
        q_send[stage, i, 0:half] = code
        q_send[stage, i, half:] = power
        link(stage, i, to).start()

    def value_of(ref, stage, i):
        return decode(ref[stage, i, 0:half], ref[stage, i, half:])

    def received(stage, i, to):
        link(stage, i, to).wait_recv()
        return value_of(q_recv, stage, i)

    def put(ref, i):
        at = pl.ds(pl.multiple_of(lax.rem(i, 2) * half, half), half)
        cols = pl.ds(pl.multiple_of(column(i // 2), block), block)
        code_ref[at, cols] = ref[3, i, 0:half]
        power_ref[pl.ds(pl.multiple_of(lax.rem(i, 2) * 16, 16), 16), cols] = ref[3, i, half:]

    def mine(i):
        return own.at[i // 2, pl.ds(pl.multiple_of(m * block + lax.rem(i, 2) * half, half), half), :]

    def load_copy(source, target):
        return pltpu.make_async_remote_copy(
            src_ref=loading.at[source], dst_ref=loading.at[source], send_sem=load_ss.at[target],
            recv_sem=load_rs.at[source], device_id={"cont": target}, device_id_type=MESH)

    def turn(u, carry):
        @pl.when(jnp.logical_and(lax.rem(u, 2) == 0, u < items))
        def _():
            t = u // 2
            slot = lax.rem(t, n_line)

            @pl.when(t >= n_line)
            def _():
                def scale_step(s, inside):
                    scale(s, slot, rows_of(s, column(t)))
                    screen((t * n_scen + s) * lines_each, lines_each)
                    return inside

                lax.fori_loop(0, n_scen, scale_step, 0)

            own[t] = jnp.dot(left[...], scaled[slot], preferred_element_type=F32)
            for h in range(2):
                send(0, u + h, to_line, own[t, pl.ds(pl.multiple_of(other * block + h * half, half), half), :])

        @pl.when(jnp.logical_and(outer, u >= 8))
        def _():
            i = u - 8
            link(3, i, to_pair).wait_recv()
            put(q_recv, i)

        @pl.when(jnp.logical_and(inner, jnp.logical_and(u >= 6, u < items + 6)))
        def _():
            i = u - 6
            far = received(2, i, to_middle)
            send(3, i, to_pair, value_of(q_send, 2, i) + far)
            put(q_send, i)

        @pl.when(jnp.logical_and(inner, jnp.logical_and(u >= 4, u < items + 4)))
        def _():
            send(2, u - 4, to_middle, mine(u - 4)[...] + received(1, u - 4, to_pair))

        @pl.when(jnp.logical_and(u >= 2, u < items + 2))
        def _():
            total = mine(u - 2)[...] + received(0, u - 2, to_line)

            @pl.when(outer)
            def _():
                send(1, u - 2, to_pair, total)

            @pl.when(inner)
            def _():
                mine(u - 2)[...] = total

        @pl.when(u == items)
        def _():
            loading[c] = jnp.maximum(jnp.abs(flow_t[...] + high[...]), jnp.abs(flow_t[...] + low[...]))
            for d in range(1, n_cont):
                load_copy(c, lax.rem(c + d, n_cont)).start()

        return carry

    lax.fori_loop(0, items + 8, turn, 0)

    for d in range(1, n_cont):
        source = lax.rem(c + d, n_cont)
        load_copy(source, source).wait_recv()
    top = loading[0]
    for k in range(1, n_cont):
        top = jnp.maximum(top, loading[k])
    worst_ref[...] = top / lim_ref[...]

    for d in range(1, n_scen):
        meta_copy(q, lax.rem(q + d, n_scen)).wait_send()
    for d in range(1, n_cont):
        load_copy(c, lax.rem(c + d, n_cont)).wait_send()

    def drain(i, carry):
        link(0, i, to_line).wait_send()

        @pl.when(outer)
        def _():
            link(1, i, to_pair).wait_send()

        @pl.when(inner)
        def _():
            link(2, i, to_middle).wait_send()
            link(3, i, to_pair).wait_send()

        return carry

    lax.fori_loop(0, items, drain, 0)


def fused(lodf, flow, out_flow, limits, ptdf_mon, ptdf_out, viol_cont, viol_line, viol_scen, rows_used):
    lines, conts = lodf.shape
    scens = flow.shape[1]
    width = ptdf_mon.shape[1]
    n_rows = viol_cont.shape[0]
    n_cont, n_line, n_scen = lax.axis_size("cont"), lax.axis_size("line"), lax.axis_size("scen")
    block = width // (n_line * n_scen)
    chunks = width // block
    half = block // 2
    items = 2 * chunks
    listed = n_scen * n_rows
    vmem = pl.BlockSpec(memory_space=pltpu.VMEM)
    dma = pltpu.SemaphoreType.DMA
    worst_t, code, power = pl.pallas_call(
        functools.partial(kernel, (n_cont, n_line, n_scen)),
        out_shape=(
            jax.ShapeDtypeStruct((scens, lines), F32),
            jax.ShapeDtypeStruct((block, width), jnp.int16),
            jax.ShapeDtypeStruct((32, width), jnp.int16),
        ),
        in_specs=[vmem] * 3 + [pl.BlockSpec(memory_space=pltpu.SMEM)] + [vmem] * 6,
        out_specs=(vmem, vmem, vmem),
        scratch_shapes=[
            pltpu.VMEM((8 * n_scen, n_rows), F32),
            pltpu.VMEM((lines, conts), F32),
            pltpu.VMEM((scens, lines), F32),
            pltpu.VMEM((scens, lines), F32),
            pltpu.VMEM((n_cont, scens, lines), F32),
            pltpu.VMEM((listed, lines + conts), BF16),
            pltpu.VMEM((listed, 128), F32),
            pltpu.VMEM((2 * block, listed), BF16),
            pltpu.VMEM((n_line, listed, block), BF16),
            pltpu.VMEM((chunks, n_line * block, block), F32),
            pltpu.VMEM((4, items, half + 16, block), jnp.int16),
            pltpu.VMEM((4, items, half + 16, block), jnp.int16),
            dma((n_scen,)), dma((n_scen,)), dma((n_cont,)), dma((n_cont,)),
            dma((4, items)), dma((4, items)),
        ],
        compiler_params=pltpu.CompilerParams(collective_id=0, has_side_effects=True, vmem_limit_bytes=56 * 1024 * 1024),
    )(
        viol_line.reshape(1, n_rows), viol_cont.reshape(1, n_rows), viol_scen.reshape(1, n_rows),
        rows_used, limits.reshape(1, lines), lodf, flow.T, out_flow, ptdf_mon, ptdf_out,
    )
    wide = 2 * block
    worst_t, schur = pl.pallas_call(
        functools.partial(finish, 1.0 / (n_rows * n_cont * n_line * n_scen)),
        grid=(width // wide,),
        out_shape=(jax.ShapeDtypeStruct((scens, lines), F32), jax.ShapeDtypeStruct((block, width), F32)),
        in_specs=[
            pl.BlockSpec((scens, lines), lambda i: (0, 0)),
            pl.BlockSpec((block, wide), lambda i: (0, i)),
            pl.BlockSpec((32, wide), lambda i: (0, i)),
        ],
        out_specs=(pl.BlockSpec((scens, lines), lambda i: (0, 0)), pl.BlockSpec((block, wide), lambda i: (0, i))),
    )(worst_t, code, power)
    return worst_t.T, schur


def local(
    lodf, flow, out_flow, limits, ptdf_mon, ptdf_out, viol_cont, viol_line, viol_scen, rows_used
):
    line_dev, cont_dev = lodf.shape
    scen_dev = flow.shape[1]
    width = ptdf_mon.shape[1]
    n_rows = viol_cont.shape[0]
    block = width // (lax.axis_size("line") * lax.axis_size("scen"))
    if (
        (lax.axis_size("cont"), lax.axis_size("line"), lax.axis_size("scen")) == (4, 2, 4)
        and line_dev == 128 and scen_dev <= 128 and scen_dev % 8 == 0
        and block % 256 == 0 and n_rows % 128 == 0 and cont_dev % 128 == 0
    ):
        return fused(
            lodf, flow, out_flow, limits, ptdf_mon, ptdf_out, viol_cont, viol_line, viol_scen, rows_used
        )
    n_cont = lax.axis_size("cont")
    n_line = lax.axis_size("line")
    n_scen = lax.axis_size("scen")
    owners = n_line * n_scen
    devices = n_cont * owners
    row_block = math.gcd(n_rows, 512)
    lines_each = math.gcd(line_dev, 32)

    def screen(pair):
        lodf_block, flow_block = pair
        post = (
            flow_block[:, :, None]
            + lodf_block.astype(jnp.float32)[:, None, :] * out_flow[None, :, :]
        )
        return jnp.max(jnp.abs(post), axis=2)

    local_worst = lax.map(
        screen,
        (
            lodf.reshape(line_dev // lines_each, lines_each, cont_dev),
            flow.reshape(line_dev // lines_each, lines_each, scen_dev),
        ),
    ).reshape(line_dev, scen_dev)
    worst = lax.pmax(local_worst, "cont") / limits[:, None]
    coef = lodf[viol_line, viol_cont].astype(jnp.float32)
    rows = (
        ptdf_mon[viol_line].astype(jnp.float32)
        + coef[:, None] * ptdf_out[viol_cont].astype(jnp.float32)
    ).astype(jnp.bfloat16)
    rows = lax.optimization_barrier(rows)
    post = flow[viol_line, viol_scen] + coef * out_flow[viol_scen, viol_cont]
    ratio = post / limits[viol_line]
    live = jnp.arange(n_rows, dtype=jnp.int32) < rows_used[0]
    weight = jnp.where(live, 1.0 + ratio * ratio, jnp.zeros_like(ratio))
    scaled = (weight[:, None] * rows.astype(jnp.float32)).astype(jnp.bfloat16)
    trips = (rows_used[0] + row_block - 1) // row_block
    row_blocks = rows.reshape(n_rows // row_block, row_block, width)
    scaled_blocks = scaled.reshape(n_rows // row_block, row_block, width)

    def step(index, acc):
        row_tile = lax.dynamic_index_in_dim(row_blocks, index, 0, keepdims=False)
        scaled_tile = lax.dynamic_index_in_dim(scaled_blocks, index, 0, keepdims=False)
        return acc + lax.dot_general(
            row_tile, scaled_tile, (((0,), (0,)), ((), ())), preferred_element_type=jnp.float32
        )

    owned = lax.psum_scatter(
        lax.fori_loop(
            0,
            trips,
            step,
            jnp.zeros((lax.axis_size(("line", "scen")) * (width // owners), width), jnp.float32),
        ),
        ("line", "scen"),
        scatter_dimension=0,
        tiled=True,
    )
    total = lax.psum(owned, "cont")
    schur = total * (1.0 / (n_rows * devices))
    return (worst, schur)


def solution(mesh):
    in_specs = (
        P("line", "cont"),
        P("line", "scen"),
        P("scen", "cont"),
        P("line"),
        P("line", None),
        P("cont", None),
        P(("cont", "line", "scen")),
        P(("cont", "line", "scen")),
        P(("cont", "line", "scen")),
        P(("cont", "line", "scen")),
    )
    out_specs = (P("line", "scen"), P(("line", "scen"), None))
    return jax.shard_map(local, mesh=mesh, in_specs=in_specs, out_specs=out_specs, check_vma=False)
```

```python
import functools
import math

import jax
import jax.numpy as jnp
from jax import lax
from jax.experimental import pallas as pl
from jax.experimental.pallas import tpu as pltpu
from jax.sharding import PartitionSpec as P


MESH = pl.DeviceIdType.MESH
F32 = jnp.float32
BF16 = jnp.bfloat16
CODE = 32760.0


def encode(x):
    top = jnp.maximum(jnp.max(jnp.abs(x), axis=0, keepdims=True), 1e-30)
    power = jnp.ceil(jnp.log2(top) + 1e-3)
    unit = x * jnp.exp2(-power)
    root = unit * lax.rsqrt(jnp.maximum(jnp.abs(unit), 1e-30)) * CODE
    code = jnp.round(root).astype(jnp.int32).astype(jnp.int16)
    power = jnp.broadcast_to(power, (16, x.shape[1])).astype(jnp.int32).astype(jnp.int16)
    return code, power


def decode(code, power, factor=1.0):
    root = code.astype(jnp.int32).astype(F32)
    unit = jnp.exp2(power.astype(jnp.int32).astype(F32)[0:1, :]) * (factor / (CODE * CODE))
    return root * jnp.abs(root) * unit


def finish(factor, worst_in, code_ref, power_ref, worst_ref, schur_ref):
    worst_ref[...] = worst_in[...]
    half = code_ref.shape[0] // 2
    for h in range(2):
        at = slice(h * half, (h + 1) * half)
        schur_ref[at, :] = decode(code_ref[at, :], power_ref[h * 16:(h + 1) * 16, :], factor)


def kernel(
    dims, line_ref, cont_ref, scen_ref, used_ref, lim_ref, lodf_ref, flow_t, out_flow_ref, mon_ref, out_ref,
    worst_ref, code_ref, power_ref,
    meta, lodf32, high, low, loading, pick, weight, left, scaled, own,
    q_send, q_recv, meta_ss, meta_rs, load_ss, load_rs, send_sems, recv_sems,
):
    n_cont, n_line, n_scen = dims
    c, m, q = lax.axis_index("cont"), lax.axis_index("line"), lax.axis_index("scen")
    pair = c + 1 - 2 * lax.rem(c, 2)
    middle = n_cont - 1 - c
    outer = jnp.logical_or(c == 0, c == n_cont - 1)
    inner = jnp.logical_not(outer)
    other = 1 - m
    n_rows = line_ref.shape[1]
    lines, width = mon_ref.shape
    conts = out_ref.shape[0]
    scens = flow_t.shape[0]
    block = code_ref.shape[0]
    chunks = width // block
    half = block // 2
    items = 2 * chunks
    parts = n_rows // 128

    barrier = pltpu.get_barrier_semaphore()
    for d in range(1, n_scen):
        pl.semaphore_signal(barrier, inc=1, device_id={"scen": lax.rem(q + d, n_scen)}, device_id_type=MESH)
    for d in range(1, n_cont):
        pl.semaphore_signal(barrier, inc=1, device_id={"cont": lax.rem(c + d, n_cont)}, device_id_type=MESH)
    pl.semaphore_signal(barrier, inc=1, device_id={"line": other}, device_id_type=MESH)

    for p in range(parts):
        at = slice(p * 128, (p + 1) * 128)
        sub = lax.broadcasted_iota(jnp.int32, (128, 128), 0)
        cols = jnp.where(sub == 0, line_ref[:, at], jnp.where(sub == 1, cont_ref[:, at], jnp.where(sub == 2, scen_ref[:, at], used_ref[0])))
        cols = jnp.transpose(cols.astype(F32))
        v_line, v_cont, v_scen, used = cols[:, 0:1], cols[:, 1:2], cols[:, 2:3], cols[:, 3:4]
        lane = lax.broadcasted_iota(jnp.int32, (128, 128), 1)
        is_line = lax.broadcasted_iota(jnp.int32, (128, lines), 1).astype(F32) == v_line
        is_cont = lax.broadcasted_iota(jnp.int32, (128, conts), 1).astype(F32) == v_cont
        is_scen = lax.broadcasted_iota(jnp.int32, (128, scens), 1).astype(F32) == v_scen
        one_line, one_scen = is_line.astype(F32), is_scen.astype(F32)
        row = jnp.dot(one_line.astype(BF16), lodf_ref[...], preferred_element_type=F32)
        coef = jnp.sum(jnp.where(is_cont, row, 0.0), axis=1, keepdims=True)
        row = jnp.dot(one_scen, flow_t[...], precision=lax.Precision.HIGHEST, preferred_element_type=F32)
        base = jnp.sum(jnp.where(is_line, row, 0.0), axis=1, keepdims=True)
        row = jnp.dot(one_scen, out_flow_ref[...], precision=lax.Precision.HIGHEST, preferred_element_type=F32)
        outage = jnp.sum(jnp.where(is_cont, row, 0.0), axis=1, keepdims=True)
        limit = jnp.sum(jnp.where(is_line, lim_ref[...], 0.0), axis=1, keepdims=True)
        ratio = (base + coef * outage) / limit
        place = lax.broadcasted_iota(jnp.int32, (128, 1), 0).astype(F32) + float(p * 128)
        w = jnp.where(place < used, 1.0 + ratio * ratio, 0.0)
        facts = jnp.where(lane == 0, v_line, jnp.where(lane == 1, v_cont, jnp.where(lane == 2, coef, jnp.where(lane == 3, w, 0.0))))
        meta[pl.ds(pl.multiple_of(q * 8, 8), 8), at] = jnp.transpose(facts)[0:8, :]

    def meta_copy(source, target):
        rows = meta.at[pl.ds(pl.multiple_of(source * 8, 8), 8), :]
        return pltpu.make_async_remote_copy(
            src_ref=rows, dst_ref=rows, send_sem=meta_ss.at[target], recv_sem=meta_rs.at[source],
            device_id={"scen": target}, device_id_type=MESH)

    pl.semaphore_wait(barrier, n_scen + n_cont - 1)
    for d in range(1, n_scen):
        meta_copy(q, lax.rem(q + d, n_scen)).start()

    lodf32[...] = lodf_ref[...].astype(F32)
    high[...] = jnp.zeros_like(high)
    low[...] = jnp.zeros_like(low)

    def pick_rows(s):
        for p in range(parts):
            facts = meta[pl.ds(pl.multiple_of(s * 8, 8), 8), p * 128:(p + 1) * 128]
            f = jnp.transpose(jnp.concatenate([facts, jnp.zeros((120, 128), F32)], axis=0))
            at = pl.ds(pl.multiple_of(s * n_rows + p * 128, 128), 128)
            lane = lax.broadcasted_iota(jnp.int32, (128, lines), 1).astype(F32)
            pick[at, 0:lines] = jnp.where(lane == f[:, 0:1], 1.0, 0.0).astype(BF16)
            lane = lax.broadcasted_iota(jnp.int32, (128, conts), 1).astype(F32)
            pick[at, lines:] = jnp.where(lane == f[:, 1:2], f[:, 2:3], 0.0).astype(BF16)
            weight[at, :] = jnp.broadcast_to(f[:, 3:4], (128, 128))

    def rows_of(s, column, count):
        at = pl.ds(pl.multiple_of(s * count, count), count)
        cols = pl.ds(pl.multiple_of(column, block), block)
        full = jnp.dot(pick[at, 0:lines], mon_ref[:, cols], preferred_element_type=F32)
        full = full + jnp.dot(pick[at, lines:], out_ref[:, cols], preferred_element_type=F32)
        return full.astype(BF16)

    def screen(first, count):
        top, bottom = high[...], low[...]
        place = lax.broadcasted_iota(jnp.int32, (scens, lines), 1)
        for i in range(count):
            factors = lodf32[pl.ds(first + i, 1), :]
            tall = short = None
            for k in range(conts // 128):
                move = out_flow_ref[:, k * 128:(k + 1) * 128] * factors[:, k * 128:(k + 1) * 128]
                tall = move if tall is None else jnp.maximum(tall, move)
                short = move if short is None else jnp.minimum(short, move)
            top = jnp.where(place == first + i, jnp.max(tall, axis=1, keepdims=True), top)
            bottom = jnp.where(place == first + i, jnp.min(short, axis=1, keepdims=True), bottom)
        high[...] = top
        low[...] = bottom

    lines_each = lines // (chunks * n_scen)

    def scale(s, slot, rows):
        count = rows.shape[0]
        at = pl.ds(pl.multiple_of(s * count, count), count)
        w = weight[at, :]
        w = jnp.concatenate([w] * (block // 128), axis=1)
        scaled[slot, at, :] = (rows.astype(F32) * w).astype(BF16)

    def column(t):
        return (lax.rem(t, n_line) * n_scen + lax.rem(q + t // n_line, n_scen)) * block

    def left_step(d, carry):
        s = lax.rem(q + d, n_scen)

        @pl.when(d > 0)
        def _():
            meta_copy(s, s).wait_recv()

        pick_rows(s)
        at = pl.ds(pl.multiple_of(s * n_rows, n_rows), n_rows)
        for line in range(n_line):
            rows = rows_of(s, column(line), n_rows)
            left[line * block:(line + 1) * block, at] = jnp.transpose(rows.astype(F32)).astype(BF16)
            scale(s, line, rows)
        screen(s * n_line * lines_each, n_line * lines_each)
        return carry

    lax.fori_loop(0, n_scen, left_step, 0)

    def link(stage, i, to):
        return pltpu.make_async_remote_copy(
            src_ref=q_send.at[stage, i], dst_ref=q_recv.at[stage, i], send_sem=send_sems.at[stage, i],
            recv_sem=recv_sems.at[stage, i], device_id=to, device_id_type=MESH)

    to_line, to_pair, to_middle = {"line": other}, {"cont": pair}, {"cont": middle}

    def send(stage, i, to, value):
        code, power = encode(value)
        q_send[stage, i, 0:half] = code
        q_send[stage, i, half:] = power
        link(stage, i, to).start()

    def value_of(ref, stage, i):
        return decode(ref[stage, i, 0:half], ref[stage, i, half:])

    def received(stage, i, to):
        link(stage, i, to).wait_recv()
        return value_of(q_recv, stage, i)

    def put(ref, i):
        at = pl.ds(pl.multiple_of(lax.rem(i, 2) * half, half), half)
        cols = pl.ds(pl.multiple_of(column(i // 2), block), block)
        code_ref[at, cols] = ref[3, i, 0:half]
        power_ref[pl.ds(pl.multiple_of(lax.rem(i, 2) * 16, 16), 16), cols] = ref[3, i, half:]

    def mine(i):
        return own.at[i // 2, pl.ds(pl.multiple_of(m * block + lax.rem(i, 2) * half, half), half), :]

    def load_copy(source, target):
        return pltpu.make_async_remote_copy(
            src_ref=loading.at[source], dst_ref=loading.at[source], send_sem=load_ss.at[target],
            recv_sem=load_rs.at[source], device_id={"cont": target}, device_id_type=MESH)

    def turn(u, carry):
        @pl.when(jnp.logical_and(lax.rem(u, 2) == 0, u < items))
        def _():
            t = u // 2
            slot = lax.rem(t, n_line)

            @pl.when(t >= n_line)
            def _():
                def scale_step(s, inside):
                    scale(s, slot, rows_of(s, column(t), 2 * n_rows))
                    screen((t * n_scen + 2 * s) * lines_each, 2 * lines_each)
                    return inside

                lax.fori_loop(0, n_scen // 2, scale_step, 0)

            own[t] = jnp.dot(left[...], scaled[slot], preferred_element_type=F32)
            for h in range(2):
                send(0, u + h, to_line, own[t, pl.ds(pl.multiple_of(other * block + h * half, half), half), :])

        @pl.when(jnp.logical_and(outer, u >= 8))
        def _():
            i = u - 8
            link(3, i, to_pair).wait_recv()
            put(q_recv, i)

        @pl.when(jnp.logical_and(inner, jnp.logical_and(u >= 6, u < items + 6)))
        def _():
            i = u - 6
            far = received(2, i, to_middle)
            send(3, i, to_pair, value_of(q_send, 2, i) + far)
            put(q_send, i)

        @pl.when(jnp.logical_and(inner, jnp.logical_and(u >= 4, u < items + 4)))
        def _():
            send(2, u - 4, to_middle, mine(u - 4)[...] + received(1, u - 4, to_pair))

        @pl.when(jnp.logical_and(u >= 2, u < items + 2))
        def _():
            total = mine(u - 2)[...] + received(0, u - 2, to_line)

            @pl.when(outer)
            def _():
                send(1, u - 2, to_pair, total)

            @pl.when(inner)
            def _():
                mine(u - 2)[...] = total

        @pl.when(u == items)
        def _():
            loading[c] = jnp.maximum(jnp.abs(flow_t[...] + high[...]), jnp.abs(flow_t[...] + low[...]))
            for d in range(1, n_cont):
                load_copy(c, lax.rem(c + d, n_cont)).start()

        return carry

    lax.fori_loop(0, items + 8, turn, 0)

    for d in range(1, n_cont):
        source = lax.rem(c + d, n_cont)
        load_copy(source, source).wait_recv()
    top = loading[0]
    for k in range(1, n_cont):
        top = jnp.maximum(top, loading[k])
    worst_ref[...] = top / lim_ref[...]

    for d in range(1, n_scen):
        meta_copy(q, lax.rem(q + d, n_scen)).wait_send()
    for d in range(1, n_cont):
        load_copy(c, lax.rem(c + d, n_cont)).wait_send()

    def drain(i, carry):
        link(0, i, to_line).wait_send()

        @pl.when(outer)
        def _():
            link(1, i, to_pair).wait_send()

        @pl.when(inner)
        def _():
            link(2, i, to_middle).wait_send()
            link(3, i, to_pair).wait_send()

        return carry

    lax.fori_loop(0, items, drain, 0)


def fused(lodf, flow, out_flow, limits, ptdf_mon, ptdf_out, viol_cont, viol_line, viol_scen, rows_used):
    lines, conts = lodf.shape
    scens = flow.shape[1]
    width = ptdf_mon.shape[1]
    n_rows = viol_cont.shape[0]
    n_cont, n_line, n_scen = lax.axis_size("cont"), lax.axis_size("line"), lax.axis_size("scen")
    block = width // (n_line * n_scen)
    chunks = width // block
    half = block // 2
    items = 2 * chunks
    listed = n_scen * n_rows
    vmem = pl.BlockSpec(memory_space=pltpu.VMEM)
    dma = pltpu.SemaphoreType.DMA
    worst_t, code, power = pl.pallas_call(
        functools.partial(kernel, (n_cont, n_line, n_scen)),
        out_shape=(
            jax.ShapeDtypeStruct((scens, lines), F32),
            jax.ShapeDtypeStruct((block, width), jnp.int16),
            jax.ShapeDtypeStruct((32, width), jnp.int16),
        ),
        in_specs=[vmem] * 3 + [pl.BlockSpec(memory_space=pltpu.SMEM)] + [vmem] * 6,
        out_specs=(vmem, vmem, vmem),
        scratch_shapes=[
            pltpu.VMEM((8 * n_scen, n_rows), F32),
            pltpu.VMEM((lines, conts), F32),
            pltpu.VMEM((scens, lines), F32),
            pltpu.VMEM((scens, lines), F32),
            pltpu.VMEM((n_cont, scens, lines), F32),
            pltpu.VMEM((listed, lines + conts), BF16),
            pltpu.VMEM((listed, 128), F32),
            pltpu.VMEM((2 * block, listed), BF16),
            pltpu.VMEM((n_line, listed, block), BF16),
            pltpu.VMEM((chunks, n_line * block, block), F32),
            pltpu.VMEM((4, items, half + 16, block), jnp.int16),
            pltpu.VMEM((4, items, half + 16, block), jnp.int16),
            dma((n_scen,)), dma((n_scen,)), dma((n_cont,)), dma((n_cont,)),
            dma((4, items)), dma((4, items)),
        ],
        compiler_params=pltpu.CompilerParams(collective_id=0, has_side_effects=True, vmem_limit_bytes=56 * 1024 * 1024),
    )(
        viol_line.reshape(1, n_rows), viol_cont.reshape(1, n_rows), viol_scen.reshape(1, n_rows),
        rows_used, limits.reshape(1, lines), lodf, flow.T, out_flow, ptdf_mon, ptdf_out,
    )
    wide = 2 * block
    worst_t, schur = pl.pallas_call(
        functools.partial(finish, 1.0 / (n_rows * n_cont * n_line * n_scen)),
        grid=(width // wide,),
        out_shape=(jax.ShapeDtypeStruct((scens, lines), F32), jax.ShapeDtypeStruct((block, width), F32)),
        in_specs=[
            pl.BlockSpec((scens, lines), lambda i: (0, 0)),
            pl.BlockSpec((block, wide), lambda i: (0, i)),
            pl.BlockSpec((32, wide), lambda i: (0, i)),
        ],
        out_specs=(pl.BlockSpec((scens, lines), lambda i: (0, 0)), pl.BlockSpec((block, wide), lambda i: (0, i))),
    )(worst_t, code, power)
    return worst_t.T, schur


def local(
    lodf, flow, out_flow, limits, ptdf_mon, ptdf_out, viol_cont, viol_line, viol_scen, rows_used
):
    line_dev, cont_dev = lodf.shape
    scen_dev = flow.shape[1]
    width = ptdf_mon.shape[1]
    n_rows = viol_cont.shape[0]
    block = width // (lax.axis_size("line") * lax.axis_size("scen"))
    if (
        (lax.axis_size("cont"), lax.axis_size("line"), lax.axis_size("scen")) == (4, 2, 4)
        and line_dev == 128 and scen_dev <= 128 and scen_dev % 8 == 0
        and block % 256 == 0 and n_rows % 128 == 0 and cont_dev % 128 == 0
    ):
        return fused(
            lodf, flow, out_flow, limits, ptdf_mon, ptdf_out, viol_cont, viol_line, viol_scen, rows_used
        )
    n_cont = lax.axis_size("cont")
    n_line = lax.axis_size("line")
    n_scen = lax.axis_size("scen")
    owners = n_line * n_scen
    devices = n_cont * owners
    row_block = math.gcd(n_rows, 512)
    lines_each = math.gcd(line_dev, 32)

    def screen(pair):
        lodf_block, flow_block = pair
        post = (
            flow_block[:, :, None]
            + lodf_block.astype(jnp.float32)[:, None, :] * out_flow[None, :, :]
        )
        return jnp.max(jnp.abs(post), axis=2)

    local_worst = lax.map(
        screen,
        (
            lodf.reshape(line_dev // lines_each, lines_each, cont_dev),
            flow.reshape(line_dev // lines_each, lines_each, scen_dev),
        ),
    ).reshape(line_dev, scen_dev)
    worst = lax.pmax(local_worst, "cont") / limits[:, None]
    coef = lodf[viol_line, viol_cont].astype(jnp.float32)
    rows = (
        ptdf_mon[viol_line].astype(jnp.float32)
        + coef[:, None] * ptdf_out[viol_cont].astype(jnp.float32)
    ).astype(jnp.bfloat16)
    rows = lax.optimization_barrier(rows)
    post = flow[viol_line, viol_scen] + coef * out_flow[viol_scen, viol_cont]
    ratio = post / limits[viol_line]
    live = jnp.arange(n_rows, dtype=jnp.int32) < rows_used[0]
    weight = jnp.where(live, 1.0 + ratio * ratio, jnp.zeros_like(ratio))
    scaled = (weight[:, None] * rows.astype(jnp.float32)).astype(jnp.bfloat16)
    trips = (rows_used[0] + row_block - 1) // row_block
    row_blocks = rows.reshape(n_rows // row_block, row_block, width)
    scaled_blocks = scaled.reshape(n_rows // row_block, row_block, width)

    def step(index, acc):
        row_tile = lax.dynamic_index_in_dim(row_blocks, index, 0, keepdims=False)
        scaled_tile = lax.dynamic_index_in_dim(scaled_blocks, index, 0, keepdims=False)
        return acc + lax.dot_general(
            row_tile, scaled_tile, (((0,), (0,)), ((), ())), preferred_element_type=jnp.float32
        )

    owned = lax.psum_scatter(
        lax.fori_loop(
            0,
            trips,
            step,
            jnp.zeros((lax.axis_size(("line", "scen")) * (width // owners), width), jnp.float32),
        ),
        ("line", "scen"),
        scatter_dimension=0,
        tiled=True,
    )
    total = lax.psum(owned, "cont")
    schur = total * (1.0 / (n_rows * devices))
    return (worst, schur)


def solution(mesh):
    in_specs = (
        P("line", "cont"),
        P("line", "scen"),
        P("scen", "cont"),
        P("line"),
        P("line", None),
        P("cont", None),
        P(("cont", "line", "scen")),
        P(("cont", "line", "scen")),
        P(("cont", "line", "scen")),
        P(("cont", "line", "scen")),
    )
    out_specs = (P("line", "scen"), P(("line", "scen"), None))
    return jax.shard_map(local, mesh=mesh, in_specs=in_specs, out_specs=out_specs, check_vma=False)
```
